32 devices in a mesh: dp: 8 (over z, x), group: 4 (over y, core).
Axes of the slice: x: 2, y: 2, z: 4, core: 2. Of those that a mesh axis runs over, the one named last changes fastest.
Arguments:
- inputs: bfloat16 [32, 256, 512], P(('dp', 'group')), may hold values from -6 to 6
- cotangent: bfloat16 [32, 256, 512], P(('dp', 'group')), may hold values from -6 to 6
- lengths: int32 [32], replicated, may hold values from 48 to 256, as said below
- square_slots: int32 [16], replicated, may hold values from 0 to 15, each once
- wide_slots: int32 [8], replicated, may hold values from 0 to 7, each once
- square_weights: bfloat16 [16, 512, 512], P('group'), may hold values from -0.25 to 0.25
- wide_weights: bfloat16 [8, 512, 2048], P('group'), may hold values from -0.25 to 0.25
- vectors: float32 [2, 48, 512], P(None, 'group'), may hold values from -1.5 to 1.5
- square_moment: float32 [16, 512, 512], P('group'), may hold values from -160 to 160
- wide_moment: float32 [8, 512, 2048], P('group'), may hold values from -160 to 160
- vector_moment: float32 [2, 48, 512], P(None, 'group'), may hold values from -28 to 28
- vector_second: float32 [2, 48, 512], P(None, 'group'), may hold values from 20.48 to 81.92
Outputs:
- block_output: bfloat16 [32, 256, 512], P(('dp', 'group'))
- input_grad: float32 [32, 256, 512], P(('dp', 'group'))
- square_moment_new: float32 [16, 512, 512], P('group')
- square_new: float32 [16, 512, 512], P('group')
- wide_moment_new: float32 [8, 512, 2048], P('group')
- wide_new: float32 [8, 512, 2048], P('group')
- vector_moment_new: float32 [2, 48, 512], P(None, 'group')
- vector_second_new: float32 [2, 48, 512], P(None, 'group')
- vector_new: float32 [2, 48, 512], P(None, 'group')
The draws below stay inside these ranges and needn't reach their ends.
Inputs may be any that keep to these rules, and one draw needn't show every extreme that they name: `lengths`: the last sequence has all 256 positions valid.
All inputs are finite; a program needn't handle non-finite values.
Results may differ from the reference program's by a relative error of at most 0.035.
Values may be sent and summed in bfloat16 or wider, within the bound.
A program may use at most 320 MiB of HBM per device.

```python
import math
import jax
import jax.numpy as jnp
from jax import lax

D = 512
F = 2048
HEADS = 8
HEAD_DIM = 64
SEQ = 256
LAYERS = 2
NS_ITERS = 5
STEP = 10
SQUARES = 16
WIDES = 8
VROWS = 48
SEQS = 32
N_DP = 8
N_GROUP = 4


def draw_lengths(key, part):
    key = jax.random.fold_in(key, 11)
    place = jnp.arange(SEQS)
    across = place // N_GROUP
    within = place % N_GROUP
    shortest = SEQ // 4
    climb = (SEQ - shortest) * (across * (N_GROUP - 1) + within * (N_DP - 1)) // (2 * (N_DP - 1) * (N_GROUP - 1))
    jitter = jax.random.randint(key, (SEQS,), 0, SEQ // 16 + 1)
    jitter = jnp.where(place == SEQS - 1, 0, jitter)
    return (shortest + climb - jitter).astype(jnp.int32)


def draw_vectors(key, part):
    key = jax.random.fold_in(key, 12)
    first, second = jax.random.split(key)
    shape = (LAYERS, VROWS, D)
    spread = jax.random.uniform(first, shape, jnp.float32, -1.0, 1.0)
    normal = jax.random.truncated_normal(second, -3.0, 3.0, shape, jnp.float32)
    row = jnp.arange(VROWS)[None, :, None]
    gains = (row < 12) & (row % 2 == 0)
    scale = jnp.where(row < 12, 0.3, jnp.where(row < 14, 0.5, jnp.where(row < 17, 0.3, 0.25)))
    return jnp.where(gains, 1.0 + 0.5 * spread, scale * normal).astype(jnp.float32)


def block_levels(own_key, dims, cuts, least, largest):
    loudness, own = 1.0, jax.random.fold_in(own_key, 6)
    for axis_at, blocks in cuts:
        heights = jnp.exp(jax.random.uniform(jax.random.fold_in(own, axis_at), (blocks,), jnp.float32, least / len(cuts), largest / len(cuts)))
        loudness = loudness * jnp.repeat(heights, dims[axis_at] // blocks).reshape([-1 if axis == axis_at else 1 for axis in range(len(dims))])
    return loudness


def normal_values(rng, extent, scale, most, cuts=(), kind=jnp.bfloat16):
    drawn = scale * jax.random.normal(rng, extent, jnp.float32)
    if cuts:
        drawn = drawn * block_levels(rng, extent, cuts, -0.22, 0.18)
    return jnp.clip(drawn, -most, most).astype(kind)


def setup_inputs(seed: int = 0) -> dict:
    key_list = jax.random.split(jax.random.key(seed), 13)
    inputs = normal_values(key_list[0], (SEQS, SEQ, D), 1.0, 6.0, ((0, 32),))
    cotangent = normal_values(key_list[1], (SEQS, SEQ, D), 1.0, 6.0, ((0, 32),))
    lengths = draw_lengths(jax.random.fold_in(key_list[12], 71), 0)
    square_slots = jax.random.permutation(key_list[3], SQUARES).astype(jnp.int32)
    wide_slots = jax.random.permutation(key_list[4], WIDES).astype(jnp.int32)
    square_weights = normal_values(key_list[5], (SQUARES, D, D), D ** -0.5, 0.25, ((0, 4),))
    wide_weights = normal_values(key_list[6], (WIDES, D, F), D ** -0.5, 0.25, ((0, 4),))
    vectors = draw_vectors(jax.random.fold_in(key_list[12], 71), 0)
    square_moment = normal_values(key_list[8], (SQUARES, D, D), (0.3 * (SEQ * N_DP * N_GROUP) ** 0.5), 160.0, ((0, 4),), jnp.float32)
    wide_moment = normal_values(key_list[9], (WIDES, D, F), (0.3 * (SEQ * N_DP * N_GROUP) ** 0.5), 160.0, ((0, 4),), jnp.float32)
    vector_moment = normal_values(key_list[10], (LAYERS, VROWS, D), (0.05 * (SEQ * N_DP * N_GROUP) ** 0.5), 28.0, ((1, 4),), jnp.float32)
    vector_second = jnp.clip(jnp.exp(math.log(81.92) - 1.3862944 * jax.random.uniform(key_list[11], (LAYERS, VROWS, D), jnp.float32) ** block_levels(key_list[11], (LAYERS, VROWS, D), ((1, 4),), -0.2, 0.2)), 20.48, 81.92)
    return dict(inputs=inputs, cotangent=cotangent, lengths=lengths, square_slots=square_slots, wide_slots=wide_slots, square_weights=square_weights, wide_weights=wide_weights, vectors=vectors, square_moment=square_moment, wide_moment=wide_moment, vector_moment=vector_moment, vector_second=vector_second)


@jax.custom_vjp
def low(v):
    return lax.optimization_barrier(v.astype(jnp.bfloat16)).astype(jnp.float32)

@jax.custom_vjp
def low_back(v):
    return v

def low_keep(v):
    return (low(v), None)

def low_pass(kept, grad):
    return (grad,)

def back_keep(v):
    return (v, None)

def back_low(kept, grad):
    return (low(grad),)
low.defvjp(low_keep, low_pass)
low_back.defvjp(back_keep, back_low)
highest = lax.Precision.HIGHEST
norm_epsilon = 1e-05
quintic_first = 3.4445
quintic_second = -4.775
quintic_third = 2.0315
momentum_decay = 0.95
muon_rate = 0.1
weight_decay = 0.01
adam_first = 0.9
adam_second = 0.99
adam_rate = 0.3
adam_epsilon = 1e-08

def layer_norm(x, gain, shift):
    middle = lax.optimization_barrier(jnp.mean(x, -1, keepdims=True))
    centred = x - middle
    spread = lax.optimization_barrier(jnp.mean(centred * centred, -1, keepdims=True))
    return centred * lax.rsqrt(spread + norm_epsilon) * gain + shift

def rel_table(rows, width):
    offset = (rows - 1 - jnp.arange(2 * rows)).astype(jnp.float32)
    freq = jnp.exp(jnp.arange(0, width, 2).astype(jnp.float32) * (-math.log(10000.0) / width))
    angle = offset[:, None] * freq[None, :]
    return jnp.stack([jnp.sin(angle), jnp.cos(angle)], axis=-1).reshape(2 * rows, width)

def shift_rel(full):
    heads, rows, cols = full.shape
    flat = full.reshape(heads, rows * cols)
    flat = flat[:, rows - 1:rows - 1 + rows * (cols - 1)]
    return flat.reshape(heads, rows, cols - 1)[:, :, :rows]

def project(left, right):
    return jnp.matmul(left, right, precision=highest)

def split_heads(value):
    return value.reshape(value.shape[0], HEADS, HEAD_DIM)

def attend(query, key_proj, value, valid, w_pos, u_bias, v_bias):
    seq_len = query.shape[0]
    position = low_back(project(low(rel_table(seq_len, D)), w_pos))
    q_con = low(query + u_bias)
    q_pos = low(query + v_bias)
    content = jnp.einsum('thd,shd->hts', split_heads(q_con), split_heads(low(key_proj)), precision=highest)
    full = jnp.einsum('thd,rhd->htr', split_heads(q_pos), split_heads(low(position)), precision=highest)
    scores = (content + shift_rel(full)) * HEAD_DIM ** (-0.5)
    scores = low_back(jnp.where(valid[None, None, :], scores, -1e+30))
    top = lax.optimization_barrier(jnp.max(scores, -1, keepdims=True))
    expo = jnp.exp(scores - top)
    probs = low(expo / lax.optimization_barrier(jnp.sum(expo, -1, keepdims=True)))
    mixed = jnp.einsum('hts,shd->thd', probs, split_heads(low(value)), precision=highest)
    return low_back(mixed.reshape(seq_len, D))

def depthwise(glu, kernel):
    width = kernel.shape[0]
    half = width // 2
    rows = glu.shape[0]
    padded = jnp.pad(glu, ((half, half), (0, 0)))
    total = jnp.zeros_like(glu)
    for tap in range(width):
        total = total + padded[tap:tap + rows] * kernel[tap]
    return total

def first_part(x, valid, mats, wides, vec):
    mask = valid[:, None]
    hidden = layer_norm(x, vec[0], vec[1])
    up_proj = low_back(project(low(hidden), wides[0]))
    down_proj = low_back(project(low(jax.nn.silu(up_proj)), wides[1].T))
    x_one = x + 0.5 * (down_proj + vec[14])
    hidden = low(layer_norm(x_one, vec[2], vec[3]))
    query = low_back(project(hidden, mats[0]))
    key_proj = low_back(project(hidden, mats[1]))
    value = low_back(project(hidden, mats[2]))
    attended = attend(query, key_proj, value, valid > 0.5, mats[4], vec[12], vec[13])
    x_two = x_one + low_back(project(low(attended), mats[3])) + vec[16]
    hidden = low(layer_norm(x_two, vec[4], vec[5]))
    gate_value = low_back(project(hidden, mats[5]))
    gate_logit = low_back(project(hidden, mats[6]))
    glu = gate_value * jax.nn.sigmoid(gate_logit) * mask
    return (x_two, depthwise(glu, vec[17:]))

def second_part(x_two, conv, valid, middle, spread, mats, wides, vec):
    mask = valid[:, None]
    normed = (conv - middle) * lax.rsqrt(spread + norm_epsilon) * vec[10] + vec[11]
    x_three = x_two + low_back(project(low(jax.nn.silu(normed)), mats[7]))
    hidden = layer_norm(x_three, vec[6], vec[7])
    up_proj = low_back(project(low(hidden), wides[2]))
    down_proj = low_back(project(low(jax.nn.silu(up_proj)), wides[3].T))
    x_four = x_three + 0.5 * (down_proj + vec[15])
    return layer_norm(x_four, vec[8], vec[9]) * mask

def block(x, masks, mats, wides, vec):
    first_ck = jax.checkpoint(first_part)
    x_two, conv = lax.map(lambda pair: first_ck(pair[0], pair[1], mats, wides, vec), (x, masks))
    count = jnp.sum(masks)
    middle = lax.optimization_barrier(jnp.sum(conv * masks[:, :, None], axis=(0, 1))) / count
    centred = conv - middle
    spread = lax.optimization_barrier(jnp.sum(centred * centred * masks[:, :, None], axis=(0, 1))) / count
    second_ck = jax.checkpoint(second_part)
    return lax.map(lambda trip: second_ck(trip[0], trip[1], trip[2], middle, spread, mats, wides, vec), (x_two, conv, masks))

def newton_schulz(matrix):
    current = matrix / (jnp.sqrt(jnp.sum(matrix * matrix)) + 1e-07)
    for sweep in range(NS_ITERS):
        low_x = current.astype(jnp.bfloat16)
        gram = jnp.dot(low_x, low_x.T, preferred_element_type=jnp.float32)
        low_gram = gram.astype(jnp.bfloat16)
        poly = quintic_second * gram + quintic_third * jnp.dot(low_gram, low_gram, preferred_element_type=jnp.float32)
        current = quintic_first * current + jnp.dot(poly.astype(jnp.bfloat16), low_x, preferred_element_type=jnp.float32)
    return current

def muon(moment, grad, weight):
    moment_new = momentum_decay * moment + grad
    looked = grad + momentum_decay * moment_new
    ortho = lax.map(newton_schulz, looked)
    scale = 0.2 * math.sqrt(max(weight.shape[1], weight.shape[2]))
    return (moment_new, weight * (1.0 - muon_rate * weight_decay) - muon_rate * scale * ortho)

def reference(inputs, cotangent, lengths, square_slots, wide_slots, square_weights, wide_weights, vectors, square_moment, wide_moment, vector_moment, vector_second):
    masks = (jnp.arange(SEQ)[None, :] < lengths[:, None]).astype(jnp.float32)

    def forward(x, squares, wides_all, vecs):
        for depth in range(LAYERS):
            mats = [squares[square_slots[8 * depth + role]] for role in range(8)]
            wides = [wides_all[wide_slots[4 * depth + role]] for role in range(4)]
            x = block(x, masks, mats, wides, vecs[depth])
        return x
    square_float = square_weights.astype(jnp.float32)
    wide_float = wide_weights.astype(jnp.float32)
    result, pull = jax.vjp(forward, inputs.astype(jnp.float32), square_float, wide_float, vectors)
    input_grad, square_grad, wide_grad, vector_grad = pull(cotangent.astype(jnp.float32))
    square_moment_new, square_new = muon(square_moment, square_grad, square_float)
    wide_moment_new, wide_new = muon(wide_moment, wide_grad, wide_float)
    moment_new = adam_first * vector_moment + (1.0 - adam_first) * vector_grad
    second_new = adam_second * vector_second + (1.0 - adam_second) * vector_grad * vector_grad
    first_hat = moment_new / (1.0 - adam_first ** STEP)
    second_hat = second_new / (1.0 - adam_second ** STEP)
    vector_new = vectors - adam_rate * first_hat / (jnp.sqrt(second_hat) + adam_epsilon)
    return (result.astype(jnp.bfloat16), input_grad, square_moment_new, square_new, wide_moment_new, wide_new, moment_new, second_new, vector_new)
```

```python
from functools import partial
import math

import jax
import jax.numpy as jnp
from jax import lax
from jax.experimental import pallas as pl
from jax.experimental.pallas import tpu as pltpu
from jax.sharding import PartitionSpec as P

D = 512
HEADS = 8
HEAD_DIM = 64
LAYERS = 2
NS_ITERS = 5
STEP = 10
SQUARES = 16
WIDES = 8


norm_epsilon = 1e-05
quintic_first = 3.4445
quintic_second = -4.775
quintic_third = 2.0315
momentum_decay = 0.95
muon_rate = 0.1
weight_decay = 0.01
adam_first = 0.9
adam_second = 0.99
adam_rate = 0.3
adam_epsilon = 1e-08


def layer_norm(x, gain, shift):
    middle = jnp.mean(x, -1, keepdims=True)
    centred = x - middle
    spread = jnp.mean(centred * centred, -1, keepdims=True)
    return centred * lax.rsqrt(spread + norm_epsilon) * gain + shift


def masked_norm(x, gain, shift, mask):
    return layer_norm(x, gain, shift) * mask


def rel_table(rows, width):
    offset = (rows - 1 - jnp.arange(2 * rows)).astype(jnp.float32)
    freq = jnp.exp(jnp.arange(0, width, 2).astype(jnp.float32) * (-math.log(10000.0) / width))
    angle = offset[:, None] * freq[None, :]
    return jnp.stack([jnp.sin(angle), jnp.cos(angle)], axis=-1).reshape(2 * rows, width)


def shift_rel(full):
    heads, rows, cols = full.shape
    flat = full.reshape(heads, rows * cols)
    flat = flat[:, rows - 1 : rows - 1 + rows * (cols - 1)]
    return flat.reshape(heads, rows, cols - 1)[:, :, :rows]


def unshift_rel(part_grad):
    heads, rows, _ = part_grad.shape
    widened = jnp.pad(part_grad, ((0, 0), (0, 0), (0, rows - 1)))
    flat = widened.reshape(heads, rows * (2 * rows - 1))
    flat = jnp.pad(flat, ((0, 0), (rows - 1, 1)))
    return flat.reshape(heads, rows, 2 * rows)


def depthwise(glu, kernel):
    width = kernel.shape[0]
    half = width // 2
    rows = glu.shape[0]
    padded = jnp.pad(glu, ((half, half), (0, 0)))
    total = jnp.zeros_like(glu)
    for tap in range(width):
        total = total + padded[tap : tap + rows] * kernel[tap]
    return total


def product(left, right):
    return jnp.dot(left, right, preferred_element_type=jnp.float32)


def cross_rows(left, right):
    return lax.dot_general(
        left, right, (((0,), (0,)), ((), ())), preferred_element_type=jnp.float32
    )


def cross_cols(left, right):
    return lax.dot_general(
        left, right, (((1,), (1,)), ((), ())), preferred_element_type=jnp.float32
    )


def split_heads(value):
    return value.reshape(value.shape[0], HEADS, -1)


def silu_slope(value):
    sig = jax.nn.sigmoid(value)
    return sig * (1.0 + value * (1.0 - sig))


def feed_forward(x, gain, shift, w_up, w_down, bias):
    hidden, pull = jax.vjp(layer_norm, x, gain, shift)
    hidden_low = hidden.astype(jnp.bfloat16)
    up_proj = product(hidden_low, w_up)
    act_low = jax.nn.silu(up_proj).astype(jnp.bfloat16)
    down_proj = cross_cols(act_low, w_down)
    return (x + 0.5 * (down_proj + bias), (pull, hidden_low, up_proj, act_low))


def feed_back(grad, kept, w_up, w_down):
    pull, hidden_low, up_proj, act_low = kept
    d_down = (0.5 * grad).astype(jnp.bfloat16)
    g_down = cross_rows(d_down, act_low)
    d_act = product(d_down, w_down)
    d_up = (d_act * silu_slope(up_proj)).astype(jnp.bfloat16)
    g_up = cross_rows(hidden_low, d_up)
    d_hidden = cross_cols(d_up, w_up)
    d_x, g_gain, g_shift = pull(d_hidden)
    return (grad + d_x, g_gain, g_shift, 0.5 * jnp.sum(grad, 0), g_up, g_down)


def scores_of(q_con, q_pos, key_low, pos_low, valid):
    content = jnp.einsum(
        "thd,shd->hts", split_heads(q_con), split_heads(key_low), preferred_element_type=jnp.float32
    )
    full = jnp.einsum(
        "thd,rhd->htr", split_heads(q_pos), split_heads(pos_low), preferred_element_type=jnp.float32
    )
    scores = (content + shift_rel(full)) * HEAD_DIM ** (-0.5)
    return jnp.where(valid[None, None, :], scores, -1e30)


def attention(x, vec, w_query, w_key, w_value, w_out, w_pos, table_low, valid):
    hidden, pull = jax.vjp(layer_norm, x, vec[2], vec[3])
    hidden_low = hidden.astype(jnp.bfloat16)
    query = product(hidden_low, w_query)
    key_low = product(hidden_low, w_key).astype(jnp.bfloat16)
    value_low = product(hidden_low, w_value).astype(jnp.bfloat16)
    pos_low = product(table_low, w_pos).astype(jnp.bfloat16)
    q_con = (query + vec[12]).astype(jnp.bfloat16)
    q_pos = (query + vec[13]).astype(jnp.bfloat16)
    scores = scores_of(q_con, q_pos, key_low, pos_low, valid)
    top = jnp.max(scores, -1, keepdims=True)
    expo = jnp.exp(scores - top)
    total = jnp.sum(expo, -1, keepdims=True)
    probs_low = (expo / total).astype(jnp.bfloat16)
    mixed = jnp.einsum(
        "hts,shd->thd", probs_low, split_heads(value_low), preferred_element_type=jnp.float32
    )
    mixed_low = mixed.reshape(x.shape[0], -1).astype(jnp.bfloat16)
    result = x + product(mixed_low, w_out) + vec[16]
    return (
        result,
        (pull, hidden_low, q_con, q_pos, key_low, value_low, pos_low, top, total, mixed_low),
    )


def attention_back(grad, kept, w_query, w_key, w_value, w_out, table_low, valid):
    pull, hidden_low, q_con, q_pos, key_low, value_low, pos_low, top, total, mixed_low = kept
    rows = grad.shape[0]
    d_out = grad.astype(jnp.bfloat16)
    g_out = cross_rows(mixed_low, d_out)
    d_mixed = split_heads(cross_cols(d_out, w_out).astype(jnp.bfloat16))
    scores = scores_of(q_con, q_pos, key_low, pos_low, valid)
    probs = jnp.exp(scores - top) / total
    probs_low = probs.astype(jnp.bfloat16)
    d_value = jnp.einsum(
        "hts,thd->shd", probs_low, d_mixed, preferred_element_type=jnp.float32
    ).reshape(rows, -1)
    d_probs = jnp.einsum(
        "thd,shd->hts", d_mixed, split_heads(value_low), preferred_element_type=jnp.float32
    )
    d_scores = probs * (d_probs - jnp.sum(probs * d_probs, -1, keepdims=True))
    d_scores = d_scores.astype(jnp.bfloat16) * HEAD_DIM ** (-0.5)
    d_con = jnp.einsum(
        "hts,shd->thd", d_scores, split_heads(key_low), preferred_element_type=jnp.float32
    ).reshape(rows, -1)
    d_key = jnp.einsum(
        "hts,thd->shd", d_scores, split_heads(q_con), preferred_element_type=jnp.float32
    ).reshape(rows, -1)
    d_full = unshift_rel(d_scores)
    d_qpos = jnp.einsum(
        "htr,rhd->thd", d_full, split_heads(pos_low), preferred_element_type=jnp.float32
    ).reshape(rows, -1)
    d_pos = jnp.einsum(
        "htr,thd->rhd", d_full, split_heads(q_pos), preferred_element_type=jnp.float32
    )
    d_pos = d_pos.reshape(2 * rows, -1).astype(jnp.bfloat16)
    g_pos = cross_rows(table_low, d_pos)
    d_query = (d_con + d_qpos).astype(jnp.bfloat16)
    d_key_low = d_key.astype(jnp.bfloat16)
    d_value_low = d_value.astype(jnp.bfloat16)
    g_query = cross_rows(hidden_low, d_query)
    g_key = cross_rows(hidden_low, d_key_low)
    g_value = cross_rows(hidden_low, d_value_low)
    d_hidden = (
        cross_cols(d_query, w_query)
        + cross_cols(d_key_low, w_key)
        + cross_cols(d_value_low, w_value)
    )
    d_x, g_gain, g_shift = pull(d_hidden)
    return (
        grad + d_x,
        g_gain,
        g_shift,
        jnp.sum(d_con, 0),
        jnp.sum(d_qpos, 0),
        jnp.sum(grad, 0),
        g_query,
        g_key,
        g_value,
        g_out,
        g_pos,
    )


def exchange_body(n_dp, n_group, reduce, x_ref, o_ref, first, second, send_one, recv_one, send_two, recv_two):
    dp, group = lax.axis_index("dp"), lax.axis_index("group")
    near = [{"dp": dp, "group": lax.rem(group + k, n_group)} for k in range(1, n_group)]
    far = [{"dp": lax.rem(dp + k, n_dp), "group": group} for k in range(1, n_dp)]
    barrier = pltpu.get_barrier_semaphore()
    for peer in near + far:
        pl.semaphore_signal(barrier, inc=1, device_id=peer, device_id_type=pl.DeviceIdType.MESH)
    pl.semaphore_wait(barrier, n_group + n_dp - 2)
    copies = []
    for k, peer in enumerate(near):
        copies.append(
            pltpu.make_async_remote_copy(
                src_ref=x_ref.at[peer["group"]] if reduce else x_ref.at[0],
                dst_ref=first.at[group],
                send_sem=send_one.at[k],
                recv_sem=recv_one.at[k],
                device_id=peer,
                device_id_type=pl.DeviceIdType.MESH,
            )
        )
        copies[-1].start()
    first[group] = x_ref[group] if reduce else x_ref[0]
    for copy in copies:
        copy.wait()
    if reduce:
        total = first[0]
        for k in range(1, n_group):
            total = total + first[k]
        second[dp] = total
    else:
        second[dp] = first[...]
    copies = []
    for k, peer in enumerate(far):
        copies.append(
            pltpu.make_async_remote_copy(
                src_ref=second.at[dp],
                dst_ref=second.at[dp],
                send_sem=send_two.at[k],
                recv_sem=recv_two.at[k],
                device_id=peer,
                device_id_type=pl.DeviceIdType.MESH,
            )
        )
        copies[-1].start()
    for copy in copies:
        copy.wait()
    if reduce:
        total = second[0]
        for k in range(1, n_dp):
            total = total + second[k]
        o_ref[...] = total
    else:
        o_ref[...] = second[...]


def exchange(x, reduce, collective_id):
    n_dp, n_group = lax.axis_size("dp"), lax.axis_size("group")
    block = x.shape[1:]
    held = (n_dp,) + block if reduce else (n_dp, n_group) + block
    return pl.pallas_call(
        partial(exchange_body, n_dp, n_group, reduce),
        out_shape=jax.ShapeDtypeStruct(block if reduce else held, x.dtype),
        in_specs=[pl.BlockSpec(memory_space=pltpu.VMEM)],
        out_specs=pl.BlockSpec(memory_space=pltpu.VMEM),
        scratch_shapes=[
            pltpu.VMEM((n_group,) + block, x.dtype),
            pltpu.VMEM(held, x.dtype),
            pltpu.SemaphoreType.DMA((n_group - 1,)),
            pltpu.SemaphoreType.DMA((n_group - 1,)),
            pltpu.SemaphoreType.DMA((n_dp - 1,)),
            pltpu.SemaphoreType.DMA((n_dp - 1,)),
        ],
        compiler_params=pltpu.CompilerParams(collective_id=collective_id, has_side_effects=True),
    )(x)


def gather_pairs(first, second):
    width = first.shape[0]
    block = jnp.stack([first, second]).reshape(1, 8, width // 4)
    return exchange(block, False, 1).reshape(-1, 2, width)


def convolution(x, vec, w_value, w_gate, w_conv, mask, count, lengths):
    hidden, pull = jax.vjp(layer_norm, x, vec[4], vec[5])
    hidden_low = hidden.astype(jnp.bfloat16)
    gate_value = product(hidden_low, w_value)
    gate_sig = jax.nn.sigmoid(product(hidden_low, w_gate))
    glu = gate_value * gate_sig * mask
    conv, conv_pull = jax.vjp(depthwise, glu, vec[17:])
    summed = jnp.sum(conv * mask, 0)
    apart = (conv - summed / jnp.sum(mask)) * mask
    pairs = gather_pairs(summed, jnp.sum(apart * apart, 0))
    numbers = lengths.astype(jnp.float32)[:, None]
    middle = jnp.sum(pairs[:, 0], 0) / count
    between = pairs[:, 0] / numbers - middle
    spread = jnp.sum(pairs[:, 1] + numbers * between * between, 0) / count
    centred = conv - middle
    inverse = lax.rsqrt(spread + norm_epsilon)
    normal = centred * inverse
    normed = normal * vec[10] + vec[11]
    act_low = jax.nn.silu(normed).astype(jnp.bfloat16)
    result = x + product(act_low, w_conv)
    return (
        result,
        (pull, hidden_low, gate_value, gate_sig, conv_pull, normal, inverse, normed, act_low),
    )


def convolution_back(grad, kept, vec, w_value, w_gate, w_conv, mask, count):
    pull, hidden_low, gate_value, gate_sig, conv_pull, normal, inverse, normed, act_low = kept
    d_out = grad.astype(jnp.bfloat16)
    g_conv = cross_rows(act_low, d_out)
    d_normed = cross_cols(d_out, w_conv) * silu_slope(normed)
    local_shift = jnp.sum(d_normed, 0)
    local_gain = jnp.sum(d_normed * normal, 0)
    pairs = gather_pairs(local_shift, local_gain)
    all_shift, all_gain = jnp.sum(pairs[:, 0], 0), jnp.sum(pairs[:, 1], 0)
    d_conv = inverse * (
        d_normed * vec[10] - mask * (vec[10] * all_shift + normal * vec[10] * all_gain) / count
    )
    d_glu, g_kernel = conv_pull(d_conv)
    d_glu = d_glu * mask
    d_value = (d_glu * gate_sig).astype(jnp.bfloat16)
    d_gate = (d_glu * gate_value * gate_sig * (1.0 - gate_sig)).astype(jnp.bfloat16)
    g_value = cross_rows(hidden_low, d_value)
    g_gate = cross_rows(hidden_low, d_gate)
    d_hidden = cross_cols(d_value, w_value) + cross_cols(d_gate, w_gate)
    d_x, g_gain, g_shift = pull(d_hidden)
    return (grad + d_x, g_gain, g_shift, local_gain, local_shift, g_kernel, g_value, g_gate, g_conv)


def muon_body(scale, moment_ref, grad_ref, weight_ref, moment_out, weight_out, current, low):
    tile = 512
    parts = [pl.ds(k, tile) for k in range(0, current.shape[1], tile)]
    total = jnp.zeros((1, 1), jnp.float32)
    for part in parts:
        grad = grad_ref[:, part].astype(jnp.float32)
        moment_new = momentum_decay * moment_ref[0, :, part] + grad
        moment_out[0, :, part] = moment_new
        looked = grad + momentum_decay * moment_new
        current[:, part] = looked
        total = total + jnp.sum(looked * looked, keepdims=True)
    factor = 1.0 / (jnp.sqrt(total) + 1e-07)
    for part in parts:
        current[:, part] = current[:, part] * factor

    def sweep(_, carry):
        gram = jnp.zeros((current.shape[0], current.shape[0]), jnp.float32)
        for part in parts:
            low[:, part] = current[:, part].astype(jnp.bfloat16)
            gram = gram + cross_cols(low[:, part], low[:, part])
        low_gram = gram.astype(jnp.bfloat16)
        poly = quintic_second * gram + quintic_third * product(low_gram, low_gram)
        poly = poly.astype(jnp.bfloat16)
        for part in parts:
            current[:, part] = quintic_first * current[:, part] + product(poly, low[:, part])
        return carry

    lax.fori_loop(0, NS_ITERS, sweep, 0)
    for part in parts:
        weight = weight_ref[0, :, part].astype(jnp.float32)
        weight_out[0, :, part] = (
            weight * (1.0 - muon_rate * weight_decay) - muon_rate * scale * current[:, part]
        )


def muon(moment, grads, weight_low, first):
    many, rows, columns = moment.shape
    scale = 0.2 * math.sqrt(max(rows, columns))
    stack = pl.BlockSpec((1, rows, columns), lambda i: (i, 0, 0))
    return pl.pallas_call(
        partial(muon_body, scale),
        grid=(many,),
        out_shape=[jax.ShapeDtypeStruct(moment.shape, jnp.float32)] * 2,
        in_specs=[stack, pl.BlockSpec((rows, columns), lambda i: (0, first + i)), stack],
        out_specs=[stack, stack],
        scratch_shapes=[
            pltpu.VMEM((rows, columns), jnp.float32),
            pltpu.VMEM((rows, columns), jnp.bfloat16),
        ],
        compiler_params=pltpu.CompilerParams(vmem_limit_bytes=56 * 1024 * 1024),
    )(moment, grads, weight_low)


def slot_order(slots):
    places = jnp.arange(slots.shape[0])
    return jnp.sum(jnp.where(slots[None, :] == places[:, None], places[None, :], 0), 1)


def per_device(
    inputs,
    cotangent,
    lengths,
    square_slots,
    wide_slots,
    square_weights,
    wide_weights,
    vectors,
    square_moment,
    wide_moment,
    vector_moment,
    vector_second,
):
    groups = lax.axis_size("group")
    me = lax.axis_index("dp") * groups + lax.axis_index("group")
    length = lax.dynamic_index_in_dim(lengths, me, keepdims=False)
    count = jnp.sum(lengths).astype(jnp.float32)
    rows = inputs.shape[1]
    valid = jnp.arange(rows) < length
    mask = valid.astype(jnp.float32)[:, None]
    all_square, all_wide = (
        lax.all_gather(square_weights, "group", axis=0, tiled=True),
        lax.all_gather(wide_weights, "group", axis=0, tiled=True),
    )
    all_vector = lax.all_gather(vectors.astype(jnp.bfloat16), "group", axis=1, tiled=True).astype(
        vectors.dtype
    )
    table_low = rel_table(rows, D).astype(jnp.bfloat16)
    x = inputs[0].astype(jnp.float32)
    saved = []
    for depth in range(LAYERS):
        mats = [all_square[square_slots[8 * depth + role]] for role in range(8)]
        wides = [all_wide[wide_slots[4 * depth + role]] for role in range(4)]
        vec = all_vector[depth]
        x, first_kept = feed_forward(x, vec[0], vec[1], wides[0], wides[1], vec[14])
        x, attend_kept = attention(
            x, vec, mats[0], mats[1], mats[2], mats[3], mats[4], table_low, valid
        )
        x, conv_kept = convolution(x, vec, mats[5], mats[6], mats[7], mask, count, lengths)
        x, second_kept = feed_forward(x, vec[6], vec[7], wides[2], wides[3], vec[15])
        x, final_pull = jax.vjp(partial(masked_norm, mask=mask), x, vec[8], vec[9])
        saved.append(
            (mats, wides, vec, first_kept, attend_kept, conv_kept, second_kept, final_pull)
        )
    block_output = x.astype(jnp.bfloat16)[None]
    grad = cotangent[0].astype(jnp.float32)
    square_list = [None] * LAYERS
    wide_list = [None] * LAYERS
    vector_list = [None] * LAYERS
    for depth in reversed(range(LAYERS)):
        mats, wides, vec, first_kept, attend_kept, conv_kept, second_kept, final_pull = saved[depth]
        grad, out_gain, out_shift = final_pull(grad)
        grad, ff2_gain, ff2_shift, ff2_bias, up_two, down_two = feed_back(
            grad, second_kept, wides[2], wides[3]
        )
        (
            grad,
            conv_gain,
            conv_shift,
            bn_gain,
            bn_shift,
            g_kernel,
            g_glu_value,
            g_glu_gate,
            g_conv,
        ) = convolution_back(grad, conv_kept, vec, mats[5], mats[6], mats[7], mask, count)
        (
            grad,
            att_gain,
            att_shift,
            g_ubias,
            g_vbias,
            att_bias,
            g_query,
            g_key,
            g_value,
            g_out,
            g_pos,
        ) = attention_back(grad, attend_kept, mats[0], mats[1], mats[2], mats[3], table_low, valid)
        grad, ff1_gain, ff1_shift, ff1_bias, up_one, down_one = feed_back(
            grad, first_kept, wides[0], wides[1]
        )
        layer_grads = [g_query, g_key, g_value, g_out, g_pos, g_glu_value, g_glu_gate, g_conv]
        layer_grads += [up_one, down_one, up_two, down_two]
        merged = jnp.concatenate([item.astype(jnp.bfloat16) for item in layer_grads], 1)
        merged = lax.psum_scatter(merged, "group", scatter_dimension=0, tiled=True)
        merged = lax.psum_scatter(merged, "dp", scatter_dimension=0, tiled=True)
        square_list[depth] = merged[:, : 8 * D].reshape(-1, 8, D)
        wide_list[depth] = merged[:, 8 * D :].reshape(-1, 4, merged.shape[1] // 6)
        vector_rows = jnp.stack(
            [
                ff1_gain,
                ff1_shift,
                att_gain,
                att_shift,
                conv_gain,
                conv_shift,
                ff2_gain,
                ff2_shift,
                out_gain,
                out_shift,
                bn_gain,
                bn_shift,
                g_ubias,
                g_vbias,
                ff1_bias,
                ff2_bias,
                att_bias,
            ]
        )
        vector_list[depth] = jnp.concatenate([vector_rows, g_kernel], 0)
    input_grad = grad[None]
    square_grad = jnp.concatenate(square_list, 1)[:, slot_order(square_slots)]
    wide_grad = jnp.concatenate(wide_list, 1)[:, slot_order(wide_slots)]
    pieces = square_grad.shape[0]
    owned = jnp.concatenate(
        [square_grad.reshape(pieces, groups, -1), wide_grad.reshape(pieces, groups, -1)], 2
    )
    owned = lax.all_to_all(owned, "group", split_axis=1, concat_axis=0)
    owned = lax.all_gather(owned, "dp", axis=1)
    owned = owned.reshape(D, -1)
    square_moment_new, square_new = muon(square_moment, owned, square_weights, 0)
    wide_moment_new, wide_new = muon(
        wide_moment, owned, wide_weights, square_moment.shape[0] * D // wide_moment.shape[2]
    )
    vector_grad = jnp.stack(vector_list)
    layers, vector_rows, width = vectors.shape
    vector_grad = vector_grad.reshape(layers, groups, vector_rows, width).swapaxes(0, 1)
    own_vector = exchange(vector_grad.reshape(groups, layers * vector_rows, width), True, 2)
    own_vector = own_vector.reshape(vectors.shape)
    moment_new = adam_first * vector_moment + (1.0 - adam_first) * own_vector
    second_new = adam_second * vector_second + (1.0 - adam_second) * own_vector * own_vector
    first_hat = moment_new / (1.0 - adam_first**STEP)
    second_hat = second_new / (1.0 - adam_second**STEP)
    vector_new = vectors - adam_rate * first_hat / (jnp.sqrt(second_hat) + adam_epsilon)
    return (
        block_output,
        input_grad,
        square_moment_new,
        square_new,
        wide_moment_new,
        wide_new,
        moment_new,
        second_new,
        vector_new,
    )


def solution(mesh):
    placed = (
        P(("dp", "group"), None, None),
        P(("dp", "group"), None, None),
        P(),
        P(),
        P(),
        P("group", None, None),
        P("group", None, None),
        P(None, "group", None),
        P("group", None, None),
        P("group", None, None),
        P(None, "group", None),
        P(None, "group", None),
    )
    return jax.shard_map(
        per_device,
        mesh=mesh,
        in_specs=placed,
        out_specs=(
            P(("dp", "group"), None, None),
            P(("dp", "group"), None, None),
            P("group", None, None),
            P("group", None, None),
            P("group", None, None),
            P("group", None, None),
            P(None, "group", None),
            P(None, "group", None),
            P(None, "group", None),
        ),
        check_vma=False,
    )
```

```python
from functools import partial
import math

import jax
import jax.numpy as jnp
from jax import lax
from jax.experimental import pallas as pl
from jax.experimental.pallas import tpu as pltpu
from jax.sharding import PartitionSpec as P

D = 512
HEADS = 8
HEAD_DIM = 64
LAYERS = 2
NS_ITERS = 5
STEP = 10
SQUARES = 16
WIDES = 8


norm_epsilon = 1e-05
quintic_first = 3.4445
quintic_second = -4.775
quintic_third = 2.0315
momentum_decay = 0.95
muon_rate = 0.1
weight_decay = 0.01
adam_first = 0.9
adam_second = 0.99
adam_rate = 0.3
adam_epsilon = 1e-08


def layer_norm(x, gain, shift):
    middle = jnp.mean(x, -1, keepdims=True)
    centred = x - middle
    spread = jnp.mean(centred * centred, -1, keepdims=True)
    return centred * lax.rsqrt(spread + norm_epsilon) * gain + shift


def masked_norm(x, gain, shift, mask):
    return layer_norm(x, gain, shift) * mask


def rel_table(rows, width):
    offset = (rows - 1 - jnp.arange(2 * rows)).astype(jnp.float32)
    freq = jnp.exp(jnp.arange(0, width, 2).astype(jnp.float32) * (-math.log(10000.0) / width))
    angle = offset[:, None] * freq[None, :]
    return jnp.stack([jnp.sin(angle), jnp.cos(angle)], axis=-1).reshape(2 * rows, width)


def shift_rel_body(full_ref, out_ref):
    rows, cols = full_ref.shape[1:]
    out_ref[0] = pltpu.roll(full_ref[0], cols - rows + 1, 1, stride=1, stride_axis=0)[:, :rows]


def shift_rel(full):
    heads, rows, cols = full.shape
    return pl.pallas_call(
        shift_rel_body,
        grid=(heads,),
        out_shape=jax.ShapeDtypeStruct((heads, rows, rows), full.dtype),
        in_specs=[pl.BlockSpec((1, rows, cols), lambda h: (h, 0, 0))],
        out_specs=pl.BlockSpec((1, rows, rows), lambda h: (h, 0, 0)),
    )(full)


def unshift_rel_body(part_ref, out_ref):
    rows = part_ref.shape[1]
    part = part_ref[0].astype(jnp.float32)
    value = jnp.concatenate([part, jnp.zeros_like(part)], 1)
    value = pltpu.roll(value, rows - 1, 1)
    turn = lax.broadcasted_iota(jnp.int32, value.shape, 0)
    step = 1
    while step < rows:
        moved = pltpu.roll(value, 2 * rows - step, 1)
        value = jnp.where((turn // step) % 2 == 1, moved, value)
        step *= 2
    out_ref[0] = value.astype(out_ref.dtype)


def unshift_rel(part_grad):
    heads, rows, _ = part_grad.shape
    return pl.pallas_call(
        unshift_rel_body,
        grid=(heads,),
        out_shape=jax.ShapeDtypeStruct((heads, rows, 2 * rows), part_grad.dtype),
        in_specs=[pl.BlockSpec((1, rows, rows), lambda h: (h, 0, 0))],
        out_specs=pl.BlockSpec((1, rows, 2 * rows), lambda h: (h, 0, 0)),
    )(part_grad)


def depthwise(glu, kernel):
    width = kernel.shape[0]
    half = width // 2
    rows = glu.shape[0]
    padded = jnp.pad(glu, ((half, half), (0, 0)))
    total = jnp.zeros_like(glu)
    for tap in range(width):
        total = total + padded[tap : tap + rows] * kernel[tap]
    return total


def product(left, right):
    return jnp.dot(left, right, preferred_element_type=jnp.float32)


def cross_rows(left, right):
    return lax.dot_general(
        left, right, (((0,), (0,)), ((), ())), preferred_element_type=jnp.float32
    )


def cross_cols(left, right):
    return lax.dot_general(
        left, right, (((1,), (1,)), ((), ())), preferred_element_type=jnp.float32
    )


def split_heads(value):
    return value.reshape(value.shape[0], HEADS, -1)


def silu_slope(value):
    sig = jax.nn.sigmoid(value)
    return sig * (1.0 + value * (1.0 - sig))


def feed_forward(x, gain, shift, w_up, w_down, bias):
    hidden, pull = jax.vjp(layer_norm, x, gain, shift)
    hidden_low = hidden.astype(jnp.bfloat16)
    up_proj = product(hidden_low, w_up)
    act_low = jax.nn.silu(up_proj).astype(jnp.bfloat16)
    down_proj = cross_cols(act_low, w_down)
    return (x + 0.5 * (down_proj + bias), (pull, hidden_low, up_proj, act_low))


def feed_back(grad, kept, w_up, w_down):
    pull, hidden_low, up_proj, act_low = kept
    d_down = (0.5 * grad).astype(jnp.bfloat16)
    g_down = cross_rows(d_down, act_low)
    d_act = product(d_down, w_down)
    d_up = (d_act * silu_slope(up_proj)).astype(jnp.bfloat16)
    g_up = cross_rows(hidden_low, d_up)
    d_hidden = cross_cols(d_up, w_up)
    d_x, g_gain, g_shift = pull(d_hidden)
    return (grad + d_x, g_gain, g_shift, 0.5 * jnp.sum(grad, 0), g_up, g_down)


def scores_of(q_con, q_pos, key_low, pos_low, valid):
    content = jnp.einsum(
        "thd,shd->hts", split_heads(q_con), split_heads(key_low), preferred_element_type=jnp.float32
    )
    full = jnp.einsum(
        "thd,rhd->htr", split_heads(q_pos), split_heads(pos_low), preferred_element_type=jnp.float32
    )
    scores = (content + shift_rel(full)) * HEAD_DIM ** (-0.5)
    return jnp.where(valid[None, None, :], scores, -1e30)


def attention(x, vec, w_query, w_key, w_value, w_out, w_pos, table_low, valid):
    hidden, pull = jax.vjp(layer_norm, x, vec[2], vec[3])
    hidden_low = hidden.astype(jnp.bfloat16)
    query = product(hidden_low, w_query)
    key_low = product(hidden_low, w_key).astype(jnp.bfloat16)
    value_low = product(hidden_low, w_value).astype(jnp.bfloat16)
    pos_low = product(table_low, w_pos).astype(jnp.bfloat16)
    q_con = (query + vec[12]).astype(jnp.bfloat16)
    q_pos = (query + vec[13]).astype(jnp.bfloat16)
    scores = scores_of(q_con, q_pos, key_low, pos_low, valid)
    top = jnp.max(scores, -1, keepdims=True)
    expo = jnp.exp(scores - top)
    total = jnp.sum(expo, -1, keepdims=True)
    probs_low = (expo / total).astype(jnp.bfloat16)
    mixed = jnp.einsum(
        "hts,shd->thd", probs_low, split_heads(value_low), preferred_element_type=jnp.float32
    )
    mixed_low = mixed.reshape(x.shape[0], -1).astype(jnp.bfloat16)
    result = x + product(mixed_low, w_out) + vec[16]
    return (
        result,
        (pull, hidden_low, q_con, q_pos, key_low, value_low, pos_low, top, total, mixed_low),
    )


def attention_back(grad, kept, w_query, w_key, w_value, w_out, table_low, valid):
    pull, hidden_low, q_con, q_pos, key_low, value_low, pos_low, top, total, mixed_low = kept
    rows = grad.shape[0]
    d_out = grad.astype(jnp.bfloat16)
    g_out = cross_rows(mixed_low, d_out)
    d_mixed = split_heads(cross_cols(d_out, w_out).astype(jnp.bfloat16))
    scores = scores_of(q_con, q_pos, key_low, pos_low, valid)
    probs = jnp.exp(scores - top) / total
    probs_low = probs.astype(jnp.bfloat16)
    d_value = jnp.einsum(
        "hts,thd->shd", probs_low, d_mixed, preferred_element_type=jnp.float32
    ).reshape(rows, -1)
    d_probs = jnp.einsum(
        "thd,shd->hts", d_mixed, split_heads(value_low), preferred_element_type=jnp.float32
    )
    d_scores = probs * (d_probs - jnp.sum(probs * d_probs, -1, keepdims=True))
    d_scores = d_scores.astype(jnp.bfloat16) * HEAD_DIM ** (-0.5)
    d_con = jnp.einsum(
        "hts,shd->thd", d_scores, split_heads(key_low), preferred_element_type=jnp.float32
    ).reshape(rows, -1)
    d_key = jnp.einsum(
        "hts,thd->shd", d_scores, split_heads(q_con), preferred_element_type=jnp.float32
    ).reshape(rows, -1)
    d_full = unshift_rel(d_scores)
    d_qpos = jnp.einsum(
        "htr,rhd->thd", d_full, split_heads(pos_low), preferred_element_type=jnp.float32
    ).reshape(rows, -1)
    d_pos = jnp.einsum(
        "htr,thd->rhd", d_full, split_heads(q_pos), preferred_element_type=jnp.float32
    )
    d_pos = d_pos.reshape(2 * rows, -1).astype(jnp.bfloat16)
    g_pos = cross_rows(table_low, d_pos)
    d_query = (d_con + d_qpos).astype(jnp.bfloat16)
    d_key_low = d_key.astype(jnp.bfloat16)
    d_value_low = d_value.astype(jnp.bfloat16)
    g_query = cross_rows(hidden_low, d_query)
    g_key = cross_rows(hidden_low, d_key_low)
    g_value = cross_rows(hidden_low, d_value_low)
    d_hidden = (
        cross_cols(d_query, w_query)
        + cross_cols(d_key_low, w_key)
        + cross_cols(d_value_low, w_value)
    )
    d_x, g_gain, g_shift = pull(d_hidden)
    return (
        grad + d_x,
        g_gain,
        g_shift,
        jnp.sum(d_con, 0),
        jnp.sum(d_qpos, 0),
        jnp.sum(grad, 0),
        g_query,
        g_key,
        g_value,
        g_out,
        g_pos,
    )


def exchange_body(n_dp, n_group, reduce, x_ref, o_ref, first, second, send_one, recv_one, send_two, recv_two):
    dp, group = lax.axis_index("dp"), lax.axis_index("group")
    near = [{"dp": dp, "group": lax.rem(group + k, n_group)} for k in range(1, n_group)]
    far = [{"dp": lax.rem(dp + k, n_dp), "group": group} for k in range(1, n_dp)]
    barrier = pltpu.get_barrier_semaphore()
    for peer in near + far:
        pl.semaphore_signal(barrier, inc=1, device_id=peer, device_id_type=pl.DeviceIdType.MESH)
    pl.semaphore_wait(barrier, n_group + n_dp - 2)
    copies = []
    for k, peer in enumerate(near):
        copies.append(
            pltpu.make_async_remote_copy(
                src_ref=x_ref.at[peer["group"]] if reduce else x_ref.at[0],
                dst_ref=first.at[group],
                send_sem=send_one.at[k],
                recv_sem=recv_one.at[k],
                device_id=peer,
                device_id_type=pl.DeviceIdType.MESH,
            )
        )
        copies[-1].start()
    first[group] = x_ref[group] if reduce else x_ref[0]
    for copy in copies:
        copy.wait()
    if reduce:
        total = first[0]
        for k in range(1, n_group):
            total = total + first[k]
        second[dp] = total
    else:
        second[dp] = first[...]
    copies = []
    for k, peer in enumerate(far):
        copies.append(
            pltpu.make_async_remote_copy(
                src_ref=second.at[dp],
                dst_ref=second.at[dp],
                send_sem=send_two.at[k],
                recv_sem=recv_two.at[k],
                device_id=peer,
                device_id_type=pl.DeviceIdType.MESH,
            )
        )
        copies[-1].start()
    for copy in copies:
        copy.wait()
    if reduce:
        total = second[0]
        for k in range(1, n_dp):
            total = total + second[k]
        o_ref[...] = total
    else:
        o_ref[...] = second[...]


def exchange(x, reduce, collective_id):
    n_dp, n_group = lax.axis_size("dp"), lax.axis_size("group")
    block = x.shape[1:]
    held = (n_dp,) + block if reduce else (n_dp, n_group) + block
    return pl.pallas_call(
        partial(exchange_body, n_dp, n_group, reduce),
        out_shape=jax.ShapeDtypeStruct(block if reduce else held, x.dtype),
        in_specs=[pl.BlockSpec(memory_space=pltpu.VMEM)],
        out_specs=pl.BlockSpec(memory_space=pltpu.VMEM),
        scratch_shapes=[
            pltpu.VMEM((n_group,) + block, x.dtype),
            pltpu.VMEM(held, x.dtype),
            pltpu.SemaphoreType.DMA((n_group - 1,)),
            pltpu.SemaphoreType.DMA((n_group - 1,)),
            pltpu.SemaphoreType.DMA((n_dp - 1,)),
            pltpu.SemaphoreType.DMA((n_dp - 1,)),
        ],
        compiler_params=pltpu.CompilerParams(collective_id=collective_id, has_side_effects=True),
    )(x)


def gather_pairs(first, second):
    width = first.shape[0]
    block = jnp.stack([first, second]).reshape(1, 8, width // 4)
    return exchange(block, False, 1).reshape(-1, 2, width)


def convolution(x, vec, w_value, w_gate, w_conv, mask, count, lengths):
    hidden, pull = jax.vjp(layer_norm, x, vec[4], vec[5])
    hidden_low = hidden.astype(jnp.bfloat16)
    gate_value = product(hidden_low, w_value)
    gate_sig = jax.nn.sigmoid(product(hidden_low, w_gate))
    glu = gate_value * gate_sig * mask
    conv, conv_pull = jax.vjp(depthwise, glu, vec[17:])
    summed = jnp.sum(conv * mask, 0)
    apart = (conv - summed / jnp.sum(mask)) * mask
    pairs = gather_pairs(summed, jnp.sum(apart * apart, 0))
    numbers = lengths.astype(jnp.float32)[:, None]
    middle = jnp.sum(pairs[:, 0], 0) / count
    between = pairs[:, 0] / numbers - middle
    spread = jnp.sum(pairs[:, 1] + numbers * between * between, 0) / count
    centred = conv - middle
    inverse = lax.rsqrt(spread + norm_epsilon)
    normal = centred * inverse
    normed = normal * vec[10] + vec[11]
    act_low = jax.nn.silu(normed).astype(jnp.bfloat16)
    result = x + product(act_low, w_conv)
    return (
        result,
        (pull, hidden_low, gate_value, gate_sig, conv_pull, normal, inverse, normed, act_low),
    )


def convolution_back(grad, kept, vec, w_value, w_gate, w_conv, mask, count):
    pull, hidden_low, gate_value, gate_sig, conv_pull, normal, inverse, normed, act_low = kept
    d_out = grad.astype(jnp.bfloat16)
    g_conv = cross_rows(act_low, d_out)
    d_normed = cross_cols(d_out, w_conv) * silu_slope(normed)
    local_shift = jnp.sum(d_normed, 0)
    local_gain = jnp.sum(d_normed * normal, 0)
    pairs = gather_pairs(local_shift, local_gain)
    all_shift, all_gain = jnp.sum(pairs[:, 0], 0), jnp.sum(pairs[:, 1], 0)
    d_conv = inverse * (
        d_normed * vec[10] - mask * (vec[10] * all_shift + normal * vec[10] * all_gain) / count
    )
    d_glu, g_kernel = conv_pull(d_conv)
    d_glu = d_glu * mask
    d_value = (d_glu * gate_sig).astype(jnp.bfloat16)
    d_gate = (d_glu * gate_value * gate_sig * (1.0 - gate_sig)).astype(jnp.bfloat16)
    g_value = cross_rows(hidden_low, d_value)
    g_gate = cross_rows(hidden_low, d_gate)
    d_hidden = cross_cols(d_value, w_value) + cross_cols(d_gate, w_gate)
    d_x, g_gain, g_shift = pull(d_hidden)
    return (grad + d_x, g_gain, g_shift, local_gain, local_shift, g_kernel, g_value, g_gate, g_conv)


def muon_body(scale, moment_ref, grad_ref, weight_ref, moment_out, weight_out, current, low):
    tile = 512
    parts = [pl.ds(k, tile) for k in range(0, current.shape[1], tile)]
    total = jnp.zeros((1, 1), jnp.float32)
    for part in parts:
        grad = grad_ref[:, part].astype(jnp.float32)
        moment_new = momentum_decay * moment_ref[0, :, part] + grad
        moment_out[0, :, part] = moment_new
        looked = grad + momentum_decay * moment_new
        current[:, part] = looked
        total = total + jnp.sum(looked * looked, keepdims=True)
    factor = 1.0 / (jnp.sqrt(total) + 1e-07)
    for part in parts:
        current[:, part] = current[:, part] * factor

    def sweep(_, carry):
        gram = jnp.zeros((current.shape[0], current.shape[0]), jnp.float32)
        for part in parts:
            low[:, part] = current[:, part].astype(jnp.bfloat16)
            gram = gram + cross_cols(low[:, part], low[:, part])
        low_gram = gram.astype(jnp.bfloat16)
        poly = quintic_second * gram + quintic_third * product(low_gram, low_gram)
        poly = poly.astype(jnp.bfloat16)
        for part in parts:
            current[:, part] = quintic_first * current[:, part] + product(poly, low[:, part])
        return carry

    lax.fori_loop(0, NS_ITERS, sweep, 0)
    for part in parts:
        weight = weight_ref[0, :, part].astype(jnp.float32)
        weight_out[0, :, part] = (
            weight * (1.0 - muon_rate * weight_decay) - muon_rate * scale * current[:, part]
        )


def muon(moment, grads, weight_low):
    many, rows, columns = moment.shape
    scale = 0.2 * math.sqrt(max(rows, columns))
    stack = pl.BlockSpec((1, rows, columns), lambda i: (i, 0, 0))
    return pl.pallas_call(
        partial(muon_body, scale),
        grid=(many,),
        out_shape=[jax.ShapeDtypeStruct(moment.shape, jnp.float32)] * 2,
        in_specs=[stack, pl.BlockSpec((rows, columns), lambda i: (0, i)), stack],
        out_specs=[stack, stack],
        scratch_shapes=[
            pltpu.VMEM((rows, columns), jnp.float32),
            pltpu.VMEM((rows, columns), jnp.bfloat16),
        ],
        compiler_params=pltpu.CompilerParams(vmem_limit_bytes=56 * 1024 * 1024),
    )(moment, grads, weight_low)


def slot_order(slots):
    places = jnp.arange(slots.shape[0])
    return jnp.sum(jnp.where(slots[None, :] == places[:, None], places[None, :], 0), 1)


def scatter_grads(grads):
    squares = sum(item.shape[1] == D for item in grads)
    merged = jnp.concatenate([item.astype(jnp.bfloat16) for item in grads], 1)
    return merged, squares


def scatter_over(merged, axis):
    return lax.psum_scatter(merged, axis, scatter_dimension=0, tiled=True)


def parted(merged, squares):
    edge = squares * D
    rows = merged.shape[0]
    return merged[:, :edge].reshape(rows, squares, D), merged[:, edge:].reshape(rows, 2, -1)


def per_device(
    inputs,
    cotangent,
    lengths,
    square_slots,
    wide_slots,
    square_weights,
    wide_weights,
    vectors,
    square_moment,
    wide_moment,
    vector_moment,
    vector_second,
):
    groups = lax.axis_size("group")
    me = lax.axis_index("dp") * groups + lax.axis_index("group")
    length = lax.dynamic_index_in_dim(lengths, me, keepdims=False)
    count = jnp.sum(lengths).astype(jnp.float32)
    rows = inputs.shape[1]
    valid = jnp.arange(rows) < length
    mask = valid.astype(jnp.float32)[:, None]
    all_square, all_wide = (
        lax.all_gather(square_weights, "group", axis=0, tiled=True),
        lax.all_gather(wide_weights, "group", axis=0, tiled=True),
    )
    all_vector = lax.all_gather(vectors.astype(jnp.bfloat16), "group", axis=1, tiled=True).astype(
        vectors.dtype
    )
    table_low = rel_table(rows, D).astype(jnp.bfloat16)
    x = inputs[0].astype(jnp.float32)
    saved = []
    for depth in range(LAYERS):
        mats = [all_square[square_slots[8 * depth + role]] for role in range(8)]
        wides = [all_wide[wide_slots[4 * depth + role]] for role in range(4)]
        vec = all_vector[depth]
        x, first_kept = feed_forward(x, vec[0], vec[1], wides[0], wides[1], vec[14])
        x, attend_kept = attention(
            x, vec, mats[0], mats[1], mats[2], mats[3], mats[4], table_low, valid
        )
        x, conv_kept = convolution(x, vec, mats[5], mats[6], mats[7], mask, count, lengths)
        x, second_kept = feed_forward(x, vec[6], vec[7], wides[2], wides[3], vec[15])
        x, final_pull = jax.vjp(partial(masked_norm, mask=mask), x, vec[8], vec[9])
        saved.append(
            (mats, wides, vec, first_kept, attend_kept, conv_kept, second_kept, final_pull)
        )
    block_output = x.astype(jnp.bfloat16)[None]
    grad = cotangent[0].astype(jnp.float32)
    square_list = [None] * LAYERS
    wide_list = [None] * LAYERS
    vector_list = [None] * LAYERS
    waiting, landed = [], []
    for depth in reversed(range(LAYERS)):
        mats, wides, vec, first_kept, attend_kept, conv_kept, second_kept, final_pull = saved[depth]
        grad, out_gain, out_shift = final_pull(grad)
        grad, ff2_gain, ff2_shift, ff2_bias, up_two, down_two = feed_back(
            grad, second_kept, wides[2], wides[3]
        )
        (
            grad,
            conv_gain,
            conv_shift,
            bn_gain,
            bn_shift,
            g_kernel,
            g_glu_value,
            g_glu_gate,
            g_conv,
        ) = convolution_back(grad, conv_kept, vec, mats[5], mats[6], mats[7], mask, count)
        merged, squares = scatter_grads([g_glu_value, g_glu_gate, g_conv, up_two, down_two])
        if landed:
            grad, merged, arrived = lax.optimization_barrier((grad, merged, landed[-1][0]))
            landed[-1] = (arrived,) + landed[-1][1:]
        else:
            grad, merged = lax.optimization_barrier((grad, merged))
        waiting.append((scatter_over(merged, "group"), depth, squares))
        (
            grad,
            att_gain,
            att_shift,
            g_ubias,
            g_vbias,
            att_bias,
            g_query,
            g_key,
            g_value,
            g_out,
            g_pos,
        ) = attention_back(grad, attend_kept, mats[0], mats[1], mats[2], mats[3], table_low, valid)
        ready, ready_depth, ready_squares = waiting.pop(0)
        grad, ready = lax.optimization_barrier((grad, ready))
        landed.append((scatter_over(ready, "dp"), ready_depth, ready_squares))
        grad, ff1_gain, ff1_shift, ff1_bias, up_one, down_one = feed_back(
            grad, first_kept, wides[0], wides[1]
        )
        merged, squares = scatter_grads([g_query, g_key, g_value, g_out, g_pos, up_one, down_one])
        if depth:
            grad, merged = lax.optimization_barrier((grad, merged))
        waiting.append((scatter_over(merged, "group"), depth, squares))
        vector_rows = jnp.stack(
            [
                ff1_gain,
                ff1_shift,
                att_gain,
                att_shift,
                conv_gain,
                conv_shift,
                ff2_gain,
                ff2_shift,
                out_gain,
                out_shift,
                bn_gain,
                bn_shift,
                g_ubias,
                g_vbias,
                ff1_bias,
                ff2_bias,
                att_bias,
            ]
        )
        vector_list[depth] = jnp.concatenate([vector_rows, g_kernel], 0)
    input_grad = grad[None]
    for merged, depth, squares in waiting:
        landed.append((scatter_over(merged, "dp"), depth, squares))
    for depth in range(LAYERS):
        parts = [parted(merged, squares) for merged, at, squares in landed if at == depth]
        square_list[depth] = jnp.concatenate([parts[1][0], parts[0][0]], 1)
        wide_list[depth] = jnp.concatenate([parts[1][1], parts[0][1]], 1)
    vector_grad = jnp.stack(vector_list)
    layers, vector_rows, width = vectors.shape
    vector_grad = vector_grad.reshape(layers, groups, vector_rows, width).swapaxes(0, 1)
    own_vector = exchange(vector_grad.reshape(groups, layers * vector_rows, width), True, 2)
    own_vector, square_grad, wide_grad = lax.optimization_barrier(
        (own_vector, jnp.concatenate(square_list, 1), jnp.concatenate(wide_list, 1))
    )
    own_vector = own_vector.reshape(vectors.shape)
    square_grad = square_grad[:, slot_order(square_slots)]
    wide_grad = wide_grad[:, slot_order(wide_slots)]
    pieces = square_grad.shape[0]
    owned = jnp.concatenate(
        [wide_grad.reshape(pieces, groups, -1), square_grad.reshape(pieces, groups, -1)], 2
    )
    owned = lax.all_to_all(owned, "group", split_axis=1, concat_axis=0)
    edge = wide_moment.shape[0] * wide_moment.shape[2]
    own_wide = lax.all_gather(owned[:, :, :edge], "dp", axis=1).reshape(D, -1)
    own_square = lax.all_gather(owned[:, :, edge:], "dp", axis=1).reshape(D, -1)
    wide_moment_new, wide_new = muon(wide_moment, own_wide, wide_weights)
    square_moment_new, square_new = muon(square_moment, own_square, square_weights)
    moment_new = adam_first * vector_moment + (1.0 - adam_first) * own_vector
    second_new = adam_second * vector_second + (1.0 - adam_second) * own_vector * own_vector
    first_hat = moment_new / (1.0 - adam_first**STEP)
    second_hat = second_new / (1.0 - adam_second**STEP)
    vector_new = vectors - adam_rate * first_hat / (jnp.sqrt(second_hat) + adam_epsilon)
    return (
        block_output,
        input_grad,
        square_moment_new,
        square_new,
        wide_moment_new,
        wide_new,
        moment_new,
        second_new,
        vector_new,
    )


def solution(mesh):
    placed = (
        P(("dp", "group"), None, None),
        P(("dp", "group"), None, None),
        P(),
        P(),
        P(),
        P("group", None, None),
        P("group", None, None),
        P(None, "group", None),
        P("group", None, None),
        P("group", None, None),
        P(None, "group", None),
        P(None, "group", None),
    )
    return jax.shard_map(
        per_device,
        mesh=mesh,
        in_specs=placed,
        out_specs=(
            P(("dp", "group"), None, None),
            P(("dp", "group"), None, None),
            P("group", None, None),
            P("group", None, None),
            P("group", None, None),
            P("group", None, None),
            P(None, "group", None),
            P(None, "group", None),
            P(None, "group", None),
        ),
        check_vma=False,
    )
```

```python
from functools import partial
import math

import jax
import jax.numpy as jnp
from jax import lax
from jax.experimental import pallas as pl
from jax.experimental.pallas import tpu as pltpu
from jax.sharding import PartitionSpec as P

D = 512
HEADS = 8
HEAD_DIM = 64
LAYERS = 2
NS_ITERS = 5
STEP = 10
SQUARES = 16
WIDES = 8


norm_epsilon = 1e-05
quintic_first = 3.4445
quintic_second = -4.775
quintic_third = 2.0315
momentum_decay = 0.95
muon_rate = 0.1
weight_decay = 0.01
adam_first = 0.9
adam_second = 0.99
adam_rate = 0.3
adam_epsilon = 1e-08


def layer_norm(x, gain, shift):
    middle = jnp.mean(x, -1, keepdims=True)
    centred = x - middle
    spread = jnp.mean(centred * centred, -1, keepdims=True)
    return centred * lax.rsqrt(spread + norm_epsilon) * gain + shift


def masked_norm(x, gain, shift, mask):
    return layer_norm(x, gain, shift) * mask


def rel_table(rows, width):
    offset = (rows - 1 - jnp.arange(2 * rows)).astype(jnp.float32)
    freq = jnp.exp(jnp.arange(0, width, 2).astype(jnp.float32) * (-math.log(10000.0) / width))
    angle = offset[:, None] * freq[None, :]
    return jnp.stack([jnp.sin(angle), jnp.cos(angle)], axis=-1).reshape(2 * rows, width)


def shift_rel_body(full_ref, out_ref):
    rows, cols = full_ref.shape[1:]
    out_ref[0] = pltpu.roll(full_ref[0], cols - rows + 1, 1, stride=1, stride_axis=0)[:, :rows]


def shift_rel(full):
    heads, rows, cols = full.shape
    return pl.pallas_call(
        shift_rel_body,
        grid=(heads,),
        out_shape=jax.ShapeDtypeStruct((heads, rows, rows), full.dtype),
        in_specs=[pl.BlockSpec((1, rows, cols), lambda h: (h, 0, 0))],
        out_specs=pl.BlockSpec((1, rows, rows), lambda h: (h, 0, 0)),
    )(full)


def unshift_rel(part_grad):
    heads, rows, _ = part_grad.shape
    widened = jnp.pad(part_grad, ((0, 0), (0, 0), (0, rows - 1)))
    flat = widened.reshape(heads, rows * (2 * rows - 1))
    flat = jnp.pad(flat, ((0, 0), (rows - 1, 1)))
    return flat.reshape(heads, rows, 2 * rows)


def depthwise(glu, kernel):
    width = kernel.shape[0]
    half = width // 2
    rows = glu.shape[0]
    padded = jnp.pad(glu, ((half, half), (0, 0)))
    total = jnp.zeros_like(glu)
    for tap in range(width):
        total = total + padded[tap : tap + rows] * kernel[tap]
    return total


def product(left, right):
    return jnp.dot(left, right, preferred_element_type=jnp.float32)


def cross_rows(left, right):
    return lax.dot_general(
        left, right, (((0,), (0,)), ((), ())), preferred_element_type=jnp.float32
    )


def cross_cols(left, right):
    return lax.dot_general(
        left, right, (((1,), (1,)), ((), ())), preferred_element_type=jnp.float32
    )


def split_heads(value):
    return value.reshape(value.shape[0], HEADS, -1)


def silu_slope(value):
    sig = jax.nn.sigmoid(value)
    return sig * (1.0 + value * (1.0 - sig))


def feed_forward(x, gain, shift, w_up, w_down, bias):
    hidden, pull = jax.vjp(layer_norm, x, gain, shift)
    hidden_low = hidden.astype(jnp.bfloat16)
    up_proj = product(hidden_low, w_up)
    act_low = jax.nn.silu(up_proj).astype(jnp.bfloat16)
    down_proj = cross_cols(act_low, w_down)
    return (x + 0.5 * (down_proj + bias), (pull, hidden_low, up_proj, act_low))


def feed_back(grad, kept, w_up, w_down):
    pull, hidden_low, up_proj, act_low = kept
    d_down = (0.5 * grad).astype(jnp.bfloat16)
    g_down = cross_rows(d_down, act_low)
    d_act = product(d_down, w_down)
    d_up = (d_act * silu_slope(up_proj)).astype(jnp.bfloat16)
    g_up = cross_rows(hidden_low, d_up)
    d_hidden = cross_cols(d_up, w_up)
    d_x, g_gain, g_shift = pull(d_hidden)
    return (grad + d_x, g_gain, g_shift, 0.5 * jnp.sum(grad, 0), g_up, g_down)


def scores_of(q_con, q_pos, key_low, pos_low, valid):
    content = jnp.einsum(
        "thd,shd->hts", split_heads(q_con), split_heads(key_low), preferred_element_type=jnp.float32
    )
    full = jnp.einsum(
        "thd,rhd->htr", split_heads(q_pos), split_heads(pos_low), preferred_element_type=jnp.float32
    )
    scores = (content + shift_rel(full)) * HEAD_DIM ** (-0.5)
    return jnp.where(valid[None, None, :], scores, -1e30)


def attention(x, vec, w_query, w_key, w_value, w_out, w_pos, table_low, valid):
    hidden, pull = jax.vjp(layer_norm, x, vec[2], vec[3])
    hidden_low = hidden.astype(jnp.bfloat16)
    query = product(hidden_low, w_query)
    key_low = product(hidden_low, w_key).astype(jnp.bfloat16)
    value_low = product(hidden_low, w_value).astype(jnp.bfloat16)
    pos_low = product(table_low, w_pos).astype(jnp.bfloat16)
    q_con = (query + vec[12]).astype(jnp.bfloat16)
    q_pos = (query + vec[13]).astype(jnp.bfloat16)
    scores = scores_of(q_con, q_pos, key_low, pos_low, valid)
    top = jnp.max(scores, -1, keepdims=True)
    expo = jnp.exp(scores - top)
    total = jnp.sum(expo, -1, keepdims=True)
    probs_low = (expo / total).astype(jnp.bfloat16)
    mixed = jnp.einsum(
        "hts,shd->thd", probs_low, split_heads(value_low), preferred_element_type=jnp.float32
    )
    mixed_low = mixed.reshape(x.shape[0], -1).astype(jnp.bfloat16)
    result = x + product(mixed_low, w_out) + vec[16]
    return (
        result,
        (pull, hidden_low, q_con, q_pos, key_low, value_low, pos_low, top, total, mixed_low),
    )


def attention_back(grad, kept, w_query, w_key, w_value, w_out, table_low, valid):
    pull, hidden_low, q_con, q_pos, key_low, value_low, pos_low, top, total, mixed_low = kept
    rows = grad.shape[0]
    d_out = grad.astype(jnp.bfloat16)
    g_out = cross_rows(mixed_low, d_out)
    d_mixed = split_heads(cross_cols(d_out, w_out).astype(jnp.bfloat16))
    scores = scores_of(q_con, q_pos, key_low, pos_low, valid)
    probs = jnp.exp(scores - top) / total
    probs_low = probs.astype(jnp.bfloat16)
    d_value = jnp.einsum(
        "hts,thd->shd", probs_low, d_mixed, preferred_element_type=jnp.float32
    ).reshape(rows, -1)
    d_probs = jnp.einsum(
        "thd,shd->hts", d_mixed, split_heads(value_low), preferred_element_type=jnp.float32
    )
    d_scores = probs * (d_probs - jnp.sum(probs * d_probs, -1, keepdims=True))
    d_scores = d_scores.astype(jnp.bfloat16) * HEAD_DIM ** (-0.5)
    d_con = jnp.einsum(
        "hts,shd->thd", d_scores, split_heads(key_low), preferred_element_type=jnp.float32
    ).reshape(rows, -1)
    d_key = jnp.einsum(
        "hts,thd->shd", d_scores, split_heads(q_con), preferred_element_type=jnp.float32
    ).reshape(rows, -1)
    d_full = unshift_rel(d_scores)
    d_qpos = jnp.einsum(
        "htr,rhd->thd", d_full, split_heads(pos_low), preferred_element_type=jnp.float32
    ).reshape(rows, -1)
    d_pos = jnp.einsum(
        "htr,thd->rhd", d_full, split_heads(q_pos), preferred_element_type=jnp.float32
    )
    d_pos = d_pos.reshape(2 * rows, -1).astype(jnp.bfloat16)
    g_pos = cross_rows(table_low, d_pos)
    d_query = (d_con + d_qpos).astype(jnp.bfloat16)
    d_key_low = d_key.astype(jnp.bfloat16)
    d_value_low = d_value.astype(jnp.bfloat16)
    g_query = cross_rows(hidden_low, d_query)
    g_key = cross_rows(hidden_low, d_key_low)
    g_value = cross_rows(hidden_low, d_value_low)
    d_hidden = (
        cross_cols(d_query, w_query)
        + cross_cols(d_key_low, w_key)
        + cross_cols(d_value_low, w_value)
    )
    d_x, g_gain, g_shift = pull(d_hidden)
    return (
        grad + d_x,
        g_gain,
        g_shift,
        jnp.sum(d_con, 0),
        jnp.sum(d_qpos, 0),
        jnp.sum(grad, 0),
        g_query,
        g_key,
        g_value,
        g_out,
        g_pos,
    )


def exchange_body(n_dp, n_group, reduce, x_ref, o_ref, first, second, send_one, recv_one, send_two, recv_two):
    dp, group = lax.axis_index("dp"), lax.axis_index("group")
    near = [{"dp": dp, "group": lax.rem(group + k, n_group)} for k in range(1, n_group)]
    far = [{"dp": lax.rem(dp + k, n_dp), "group": group} for k in range(1, n_dp)]
    barrier = pltpu.get_barrier_semaphore()
    for peer in near + far:
        pl.semaphore_signal(barrier, inc=1, device_id=peer, device_id_type=pl.DeviceIdType.MESH)
    pl.semaphore_wait(barrier, n_group + n_dp - 2)
    copies = []
    for k, peer in enumerate(near):
        copies.append(
            pltpu.make_async_remote_copy(
                src_ref=x_ref.at[peer["group"]] if reduce else x_ref.at[0],
                dst_ref=first.at[group],
                send_sem=send_one.at[k],
                recv_sem=recv_one.at[k],
                device_id=peer,
                device_id_type=pl.DeviceIdType.MESH,
            )
        )
        copies[-1].start()
    first[group] = x_ref[group] if reduce else x_ref[0]
    for copy in copies:
        copy.wait()
    if reduce:
        total = first[0]
        for k in range(1, n_group):
            total = total + first[k]
        second[dp] = total
    else:
        second[dp] = first[...]
    copies = []
    for k, peer in enumerate(far):
        copies.append(
            pltpu.make_async_remote_copy(
                src_ref=second.at[dp],
                dst_ref=second.at[dp],
                send_sem=send_two.at[k],
                recv_sem=recv_two.at[k],
                device_id=peer,
                device_id_type=pl.DeviceIdType.MESH,
            )
        )
        copies[-1].start()
    for copy in copies:
        copy.wait()
    if reduce:
        total = second[0]
        for k in range(1, n_dp):
            total = total + second[k]
        o_ref[...] = total
    else:
        o_ref[...] = second[...]


def exchange(x, reduce, collective_id):
    n_dp, n_group = lax.axis_size("dp"), lax.axis_size("group")
    block = x.shape[1:]
    held = (n_dp,) + block if reduce else (n_dp, n_group) + block
    return pl.pallas_call(
        partial(exchange_body, n_dp, n_group, reduce),
        out_shape=jax.ShapeDtypeStruct(block if reduce else held, x.dtype),
        in_specs=[pl.BlockSpec(memory_space=pltpu.VMEM)],
        out_specs=pl.BlockSpec(memory_space=pltpu.VMEM),
        scratch_shapes=[
            pltpu.VMEM((n_group,) + block, x.dtype),
            pltpu.VMEM(held, x.dtype),
            pltpu.SemaphoreType.DMA((n_group - 1,)),
            pltpu.SemaphoreType.DMA((n_group - 1,)),
            pltpu.SemaphoreType.DMA((n_dp - 1,)),
            pltpu.SemaphoreType.DMA((n_dp - 1,)),
        ],
        compiler_params=pltpu.CompilerParams(collective_id=collective_id, has_side_effects=True),
    )(x)


def gather_pairs(first, second):
    width = first.shape[0]
    block = jnp.stack([first, second]).reshape(1, 8, width // 4)
    return exchange(block, False, 1).reshape(-1, 2, width)


def convolution(x, vec, w_value, w_gate, w_conv, mask, count, lengths):
    hidden, pull = jax.vjp(layer_norm, x, vec[4], vec[5])
    hidden_low = hidden.astype(jnp.bfloat16)
    gate_value = product(hidden_low, w_value)
    gate_sig = jax.nn.sigmoid(product(hidden_low, w_gate))
    glu = gate_value * gate_sig * mask
    conv, conv_pull = jax.vjp(depthwise, glu, vec[17:])
    summed = jnp.sum(conv * mask, 0)
    apart = (conv - summed / jnp.sum(mask)) * mask
    pairs = gather_pairs(summed, jnp.sum(apart * apart, 0))
    numbers = lengths.astype(jnp.float32)[:, None]
    middle = jnp.sum(pairs[:, 0], 0) / count
    between = pairs[:, 0] / numbers - middle
    spread = jnp.sum(pairs[:, 1] + numbers * between * between, 0) / count
    centred = conv - middle
    inverse = lax.rsqrt(spread + norm_epsilon)
    normal = centred * inverse
    normed = normal * vec[10] + vec[11]
    act_low = jax.nn.silu(normed).astype(jnp.bfloat16)
    result = x + product(act_low, w_conv)
    return (
        result,
        (pull, hidden_low, gate_value, gate_sig, conv_pull, normal, inverse, normed, act_low),
    )


def convolution_back(grad, kept, vec, w_value, w_gate, w_conv, mask, count):
    pull, hidden_low, gate_value, gate_sig, conv_pull, normal, inverse, normed, act_low = kept
    d_out = grad.astype(jnp.bfloat16)
    g_conv = cross_rows(act_low, d_out)
    d_normed = cross_cols(d_out, w_conv) * silu_slope(normed)
    local_shift = jnp.sum(d_normed, 0)
    local_gain = jnp.sum(d_normed * normal, 0)
    pairs = gather_pairs(local_shift, local_gain)
    all_shift, all_gain = jnp.sum(pairs[:, 0], 0), jnp.sum(pairs[:, 1], 0)
    d_conv = inverse * (
        d_normed * vec[10] - mask * (vec[10] * all_shift + normal * vec[10] * all_gain) / count
    )
    d_glu, g_kernel = conv_pull(d_conv)
    d_glu = d_glu * mask
    d_value = (d_glu * gate_sig).astype(jnp.bfloat16)
    d_gate = (d_glu * gate_value * gate_sig * (1.0 - gate_sig)).astype(jnp.bfloat16)
    g_value = cross_rows(hidden_low, d_value)
    g_gate = cross_rows(hidden_low, d_gate)
    d_hidden = cross_cols(d_value, w_value) + cross_cols(d_gate, w_gate)
    d_x, g_gain, g_shift = pull(d_hidden)
    return (grad + d_x, g_gain, g_shift, local_gain, local_shift, g_kernel, g_value, g_gate, g_conv)


def muon_body(scale, moment_ref, grad_ref, weight_ref, moment_out, weight_out, current, low):
    tile = 512
    parts = [pl.ds(k, tile) for k in range(0, current.shape[1], tile)]
    total = jnp.zeros((1, 1), jnp.float32)
    for part in parts:
        grad = grad_ref[:, part].astype(jnp.float32)
        moment_new = momentum_decay * moment_ref[0, :, part] + grad
        moment_out[0, :, part] = moment_new
        looked = grad + momentum_decay * moment_new
        current[:, part] = looked
        total = total + jnp.sum(looked * looked, keepdims=True)
    factor = 1.0 / (jnp.sqrt(total) + 1e-07)
    for part in parts:
        current[:, part] = current[:, part] * factor

    def sweep(_, carry):
        gram = jnp.zeros((current.shape[0], current.shape[0]), jnp.float32)
        for part in parts:
            low[:, part] = current[:, part].astype(jnp.bfloat16)
            gram = gram + cross_cols(low[:, part], low[:, part])
        low_gram = gram.astype(jnp.bfloat16)
        poly = quintic_second * gram + quintic_third * product(low_gram, low_gram)
        poly = poly.astype(jnp.bfloat16)
        for part in parts:
            current[:, part] = quintic_first * current[:, part] + product(poly, low[:, part])
        return carry

    lax.fori_loop(0, NS_ITERS, sweep, 0)
    for part in parts:
        weight = weight_ref[0, :, part].astype(jnp.float32)
        weight_out[0, :, part] = (
            weight * (1.0 - muon_rate * weight_decay) - muon_rate * scale * current[:, part]
        )


def muon(moment, grads, weight_low, first):
    many, rows, columns = moment.shape
    scale = 0.2 * math.sqrt(max(rows, columns))
    stack = pl.BlockSpec((1, rows, columns), lambda i: (i, 0, 0))
    return pl.pallas_call(
        partial(muon_body, scale),
        grid=(many,),
        out_shape=[jax.ShapeDtypeStruct(moment.shape, jnp.float32)] * 2,
        in_specs=[stack, pl.BlockSpec((rows, columns), lambda i: (0, first + i)), stack],
        out_specs=[stack, stack],
        scratch_shapes=[
            pltpu.VMEM((rows, columns), jnp.float32),
            pltpu.VMEM((rows, columns), jnp.bfloat16),
        ],
        compiler_params=pltpu.CompilerParams(vmem_limit_bytes=56 * 1024 * 1024),
    )(moment, grads, weight_low)


def slot_order(slots):
    places = jnp.arange(slots.shape[0])
    return jnp.sum(jnp.where(slots[None, :] == places[:, None], places[None, :], 0), 1)


def merge_grads(grads):
    return jnp.concatenate([item.astype(jnp.bfloat16) for item in grads], 1)


def scatter_over(merged, axis):
    return lax.psum_scatter(merged, axis, scatter_dimension=0, tiled=True)


def per_device(
    inputs,
    cotangent,
    lengths,
    square_slots,
    wide_slots,
    square_weights,
    wide_weights,
    vectors,
    square_moment,
    wide_moment,
    vector_moment,
    vector_second,
):
    groups = lax.axis_size("group")
    me = lax.axis_index("dp") * groups + lax.axis_index("group")
    length = lax.dynamic_index_in_dim(lengths, me, keepdims=False)
    count = jnp.sum(lengths).astype(jnp.float32)
    rows = inputs.shape[1]
    valid = jnp.arange(rows) < length
    mask = valid.astype(jnp.float32)[:, None]
    all_square, all_wide = (
        lax.all_gather(square_weights, "group", axis=0, tiled=True),
        lax.all_gather(wide_weights, "group", axis=0, tiled=True),
    )
    all_vector = lax.all_gather(vectors.astype(jnp.bfloat16), "group", axis=1, tiled=True).astype(
        vectors.dtype
    )
    table_low = rel_table(rows, D).astype(jnp.bfloat16)
    x = inputs[0].astype(jnp.float32)
    saved = []
    for depth in range(LAYERS):
        mats = [all_square[square_slots[8 * depth + role]] for role in range(8)]
        wides = [all_wide[wide_slots[4 * depth + role]] for role in range(4)]
        vec = all_vector[depth]
        x, first_kept = feed_forward(x, vec[0], vec[1], wides[0], wides[1], vec[14])
        x, attend_kept = attention(
            x, vec, mats[0], mats[1], mats[2], mats[3], mats[4], table_low, valid
        )
        x, conv_kept = convolution(x, vec, mats[5], mats[6], mats[7], mask, count, lengths)
        x, second_kept = feed_forward(x, vec[6], vec[7], wides[2], wides[3], vec[15])
        x, final_pull = jax.vjp(partial(masked_norm, mask=mask), x, vec[8], vec[9])
        saved.append(
            (mats, wides, vec, first_kept, attend_kept, conv_kept, second_kept, final_pull)
        )
    block_output = x.astype(jnp.bfloat16)[None]
    grad = cotangent[0].astype(jnp.float32)
    square_list = [None] * LAYERS
    wide_list = [None] * LAYERS
    vector_list = [None] * LAYERS
    waiting, landed = [], []
    for depth in reversed(range(LAYERS)):
        mats, wides, vec, first_kept, attend_kept, conv_kept, second_kept, final_pull = saved[depth]
        grad, out_gain, out_shift = final_pull(grad)
        grad, ff2_gain, ff2_shift, ff2_bias, up_two, down_two = feed_back(
            grad, second_kept, wides[2], wides[3]
        )
        (
            grad,
            conv_gain,
            conv_shift,
            bn_gain,
            bn_shift,
            g_kernel,
            g_glu_value,
            g_glu_gate,
            g_conv,
        ) = convolution_back(grad, conv_kept, vec, mats[5], mats[6], mats[7], mask, count)
        (
            grad,
            att_gain,
            att_shift,
            g_ubias,
            g_vbias,
            att_bias,
            g_query,
            g_key,
            g_value,
            g_out,
            g_pos,
        ) = attention_back(grad, attend_kept, mats[0], mats[1], mats[2], mats[3], table_low, valid)
        if waiting:
            grad, ready = lax.optimization_barrier((grad, waiting.pop()))
            landed.append(scatter_over(ready, "dp"))
        grad, ff1_gain, ff1_shift, ff1_bias, up_one, down_one = feed_back(
            grad, first_kept, wides[0], wides[1]
        )
        merged = merge_grads(
            [g_query, g_key, g_value, g_out, g_pos, g_glu_value, g_glu_gate, g_conv]
            + [up_one, down_one, up_two, down_two]
        )
        if depth:
            grad, merged = lax.optimization_barrier((grad, merged))
        else:
            merged, landed[0] = lax.optimization_barrier((merged, landed[0]))
        waiting.append(scatter_over(merged, "group"))
        vector_rows = jnp.stack(
            [
                ff1_gain,
                ff1_shift,
                att_gain,
                att_shift,
                conv_gain,
                conv_shift,
                ff2_gain,
                ff2_shift,
                out_gain,
                out_shift,
                bn_gain,
                bn_shift,
                g_ubias,
                g_vbias,
                ff1_bias,
                ff2_bias,
                att_bias,
            ]
        )
        vector_list[depth] = jnp.concatenate([vector_rows, g_kernel], 0)
    input_grad = grad[None]
    landed.append(scatter_over(waiting.pop(), "dp"))
    for depth, merged in enumerate(reversed(landed)):
        rows = merged.shape[0]
        square_list[depth] = merged[:, : 8 * D].reshape(rows, 8, D)
        wide_list[depth] = merged[:, 8 * D :].reshape(rows, 4, -1)
    vector_grad = jnp.stack(vector_list)
    layers, vector_rows, width = vectors.shape
    vector_grad = vector_grad.reshape(layers, groups, vector_rows, width).swapaxes(0, 1)
    own_vector = exchange(vector_grad.reshape(groups, layers * vector_rows, width), True, 2)
    own_vector, square_grad, wide_grad = lax.optimization_barrier(
        (own_vector, jnp.concatenate(square_list, 1), jnp.concatenate(wide_list, 1))
    )
    own_vector = own_vector.reshape(vectors.shape)
    square_grad = square_grad[:, slot_order(square_slots)]
    wide_grad = wide_grad[:, slot_order(wide_slots)]
    pieces = square_grad.shape[0]
    owned = jnp.concatenate(
        [wide_grad.reshape(pieces, groups, -1), square_grad.reshape(pieces, groups, -1)], 2
    )
    owned = lax.all_to_all(owned, "group", split_axis=1, concat_axis=0)
    edge = wide_moment.shape[0] * wide_moment.shape[2]
    owned = lax.all_gather(owned, "dp", axis=1).reshape(D, -1)
    wide_moment_new, wide_new = muon(wide_moment, owned, wide_weights, 0)
    square_moment_new, square_new = muon(
        square_moment, owned, square_weights, edge // D
    )
    moment_new = adam_first * vector_moment + (1.0 - adam_first) * own_vector
    second_new = adam_second * vector_second + (1.0 - adam_second) * own_vector * own_vector
    first_hat = moment_new / (1.0 - adam_first**STEP)
    second_hat = second_new / (1.0 - adam_second**STEP)
    vector_new = vectors - adam_rate * first_hat / (jnp.sqrt(second_hat) + adam_epsilon)
    return (
        block_output,
        input_grad,
        square_moment_new,
        square_new,
        wide_moment_new,
        wide_new,
        moment_new,
        second_new,
        vector_new,
    )


def solution(mesh):
    placed = (
        P(("dp", "group"), None, None),
        P(("dp", "group"), None, None),
        P(),
        P(),
        P(),
        P("group", None, None),
        P("group", None, None),
        P(None, "group", None),
        P("group", None, None),
        P("group", None, None),
        P(None, "group", None),
        P(None, "group", None),
    )
    return jax.shard_map(
        per_device,
        mesh=mesh,
        in_specs=placed,
        out_specs=(
            P(("dp", "group"), None, None),
            P(("dp", "group"), None, None),
            P("group", None, None),
            P("group", None, None),
            P("group", None, None),
            P("group", None, None),
            P(None, "group", None),
            P(None, "group", None),
            P(None, "group", None),
        ),
        check_vma=False,
    )
```
